128 devices in a mesh: dp: 8 (over x_hi, y), tm: 8 (over z, core), height: 2 (over x_lo).
Axes of the slice: x: 4 (x_hi: 2, x_lo: 2; x = x_hi * 2 + x_lo), y: 4, z: 4, core: 2. Of those that a mesh axis runs over, the one named last changes fastest.
Arguments:
- block_input: bfloat16 [8, 16, 16, 64, 384], P('dp', 'tm', 'height'), may hold values from -6 to 6
- block_output: bfloat16 [8, 16, 16, 64, 384], P('dp', None, 'height', 'tm'), may hold values from -6 to 6
- latent_grad: float32 [8, 16, 16, 1024], P('dp', None, 'height', 'tm'), may hold values from -6 to 6
- seeds: int32 [8], P('dp'), may hold values from 0 to 29999
- lengths: int32 [8], P('dp'), may hold values from 1 to 16, as said below
- conv_weight: bfloat16 [384, 27, 384], P(('dp', 'tm', 'height')), may hold values from -0.0625 to 0.0625
- head_weight: bfloat16 [384, 32], replicated, may hold values from -0.3125 to 0.3125
Outputs:
- input_grad: bfloat16 [8, 16, 16, 64, 384], P('dp', 'tm', 'height')
- conv_grad: float32 [384, 27, 384], P(('dp', 'tm', 'height'))
- head_grad: float32 [384, 32], P(('dp', 'tm', 'height'))
The draws below stay inside these ranges and needn't reach their ends.
Inputs may be any that keep to these rules, and one draw needn't show every extreme that they name: `lengths`: some clip has all 16 frames valid in every draw.
All inputs are finite; a program needn't handle non-finite values.
Results may differ from the reference program's by a relative error of at most 0.0075.
Values may be sent and summed in bfloat16 or wider, within the bound.
A program may use at most 192 MiB of HBM per device.

```python
import math
import jax
import jax.numpy as jnp
from jax import lax

C = 384
Z = 16
BATCH = 8
FRAMES = 16
H = 16
W = 64


def draw_lengths(key, part):
    key = jax.random.fold_in(key, 5)
    length_key, pick_key = jax.random.split(key)
    drawn = jax.random.randint(length_key, (BATCH,), 1, FRAMES + 1)
    chosen = jax.random.randint(pick_key, (), 0, BATCH)
    return jnp.where(jnp.arange(BATCH) == chosen, FRAMES, drawn).astype(jnp.int32)


def plant(entries, rng, smallest, largest):
    longest = entries.shape.index(max(entries.shape))
    spots = []
    for shift in (0, 1):
        where = [jax.random.randint(jax.random.fold_in(rng, axis), (), 0, length) for axis, length in enumerate(entries.shape)]
        where[longest] = (where[longest] + shift) % entries.shape[longest]
        spots.append(tuple(where))
    return entries.at[spots[0]].set(smallest).at[spots[1]].set(largest)


def shard_levels(own_key, shape, pieces, least, largest):
    gain, own = 1.0, jax.random.fold_in(own_key, 6)
    for dim, shards_of in pieces:
        draws = jnp.exp(jax.random.uniform(jax.random.fold_in(own, dim), (shards_of,), jnp.float32, least / len(pieces), largest / len(pieces)))
        gain = gain * jnp.repeat(draws, shape[dim] // shards_of).reshape([-1 if axis == dim else 1 for axis in range(len(shape))])
    return gain


def normal_values(stream_key, extent, deviation, reach, cuts=(), held_as=jnp.bfloat16):
    factor_of = shard_levels(stream_key, extent, cuts, -0.22, 0.18) if cuts else 1.0
    values = jax.random.normal(stream_key, extent, jnp.float32) * deviation * factor_of
    return jnp.minimum(jnp.maximum(values, -reach), reach).astype(held_as)


def setup_inputs(seed: int = 0) -> dict:
    arg_keys = jax.random.split(jax.random.key(seed), 8)
    block_input = normal_values(arg_keys[0], (BATCH, FRAMES, H, W, C), 1.0, 6.0, ((0, 8), (1, 8), (2, 2)))
    block_output = normal_values(arg_keys[1], (BATCH, FRAMES, H, W, C), 1.0, 6.0, ((0, 8), (2, 2), (3, 8)))
    latent_grad = normal_values(arg_keys[2], (BATCH, FRAMES, H, W * Z), 1.0, 6.0, ((0, 8), (2, 2), (3, 8)), jnp.float32)
    seeds = plant(jax.random.randint(arg_keys[3], (BATCH,), 0, 30000), jax.random.fold_in(arg_keys[3], 1), 0, 29999).astype(jnp.int32)
    lengths = draw_lengths(jax.random.fold_in(arg_keys[7], 71), 0)
    conv_weight = normal_values(arg_keys[5], (C, 27, C), (27 * C) ** -0.5, 0.0625, ((0, 128),))
    head_weight = normal_values(arg_keys[6], (C, 2 * Z), C ** -0.5, 0.3125)
    return dict(block_input=block_input, block_output=block_output, latent_grad=latent_grad, seeds=seeds, lengths=lengths, conv_weight=conv_weight, head_weight=head_weight)


EPSILON = 1e-06
ROOT_THREE = math.sqrt(3.0)
OFFSETS = [(frame_off, row_off, col_off) for frame_off in range(3) for row_off in range(3) for col_off in range(3)]

def silu_slope(values):
    logistic = jax.nn.sigmoid(values)
    return logistic * (1.0 + values * (1.0 - logistic))

def norm_back(grad_in, normed, inverse):
    return inverse * (grad_in - normed * lax.optimization_barrier(jnp.mean(grad_in * normed, axis=-1, keepdims=True)))

def unit_noise(seed_value, position):
    primary = (seed_value * 7919 + position) % 30269
    primary = (primary * primary + 7) % 30269
    primary = (primary * primary + 101) % 30269
    secondary = (seed_value * 7907 + position * 3) % 30307
    secondary = (secondary * secondary + 13) % 30307
    secondary = (secondary * secondary + 211) % 30307
    combined = (primary + secondary) % 30269
    return ROOT_THREE * ((combined.astype(jnp.float32) + 0.5) * (2.0 / 30269.0) - 1.0)

def reference(block_input, block_output, latent_grad, seeds, lengths, conv_weight, head_weight):
    cell_count = FRAMES * H * W
    scaling = 1.0 / math.sqrt(BATCH * FRAMES * H * W)
    frame_ids = jnp.arange(FRAMES, dtype=jnp.int32)[:, None, None, None]
    row_ids = jnp.arange(H, dtype=jnp.int32)[None, :, None, None]
    col_ids = jnp.arange(W, dtype=jnp.int32)[None, None, :, None]
    chan_ids = jnp.arange(Z, dtype=jnp.int32)[None, None, None, :]
    position = (((frame_ids * H + row_ids) * W + col_ids) * Z + chan_ids).reshape(cell_count, Z)

    def one_clip(carry, item):
        inputs, outputs, upstream, seed_value, length = item
        input_f = inputs.astype(jnp.float32)
        inverse_in = lax.rsqrt(lax.optimization_barrier(jnp.mean(input_f * input_f, axis=-1, keepdims=True)) + EPSILON)
        normed_in = input_f * inverse_in
        active = jax.nn.silu(normed_in).astype(jnp.bfloat16)
        output_f = outputs.astype(jnp.float32).reshape(cell_count, C)
        inverse_out = lax.rsqrt(lax.optimization_barrier(jnp.mean(output_f * output_f, axis=-1, keepdims=True)) + EPSILON)
        normed_out = output_f * inverse_out
        active_out = jax.nn.silu(normed_out).astype(jnp.bfloat16)
        latent = jnp.dot(active_out, head_weight, preferred_element_type=jnp.float32)
        mean_part = latent[:, :Z]
        logvar = latent[:, Z:]
        noise = unit_noise(seed_value, position)
        frame_valid = jnp.broadcast_to((jnp.arange(FRAMES, dtype=jnp.int32) < length)[:, None, None, None], (FRAMES, H, W, 1))
        frame_valid = frame_valid.reshape(cell_count, 1).astype(jnp.float32)
        upstream_f = upstream.reshape(cell_count, Z)
        grad_mean = frame_valid * (upstream_f + mean_part)
        grad_logvar = frame_valid * (0.5 * upstream_f * noise * jnp.exp(0.5 * logvar) + 0.5 * (jnp.exp(logvar) - 1.0))
        head_in = jnp.concatenate([grad_mean, grad_logvar], axis=1).astype(jnp.bfloat16)
        grad_active = jnp.dot(head_in, head_weight.T, preferred_element_type=jnp.float32)
        grad_sum = norm_back(grad_active * silu_slope(normed_out), normed_out, inverse_out)
        grad_conv = grad_sum.astype(jnp.bfloat16)
        padded_act = jnp.pad(active, ((2, 0), (1, 1), (1, 1), (0, 0)))
        padded_grad = jnp.pad(grad_conv.reshape(FRAMES, H, W, C), ((0, 2), (1, 1), (1, 1), (0, 0)))
        conv_terms = []
        grad_act = jnp.zeros((cell_count, C), jnp.float32)
        for number, offset in enumerate(OFFSETS):
            window = padded_act[offset[0]:offset[0] + FRAMES, offset[1]:offset[1] + H, offset[2]:offset[2] + W].reshape(cell_count, C)
            conv_terms.append(jnp.dot(window.T, grad_conv, preferred_element_type=jnp.float32))
            back_window = padded_grad[2 - offset[0]:2 - offset[0] + FRAMES, 2 - offset[1]:2 - offset[1] + H, 2 - offset[2]:2 - offset[2] + W].reshape(cell_count, C)
            grad_act = grad_act + jnp.dot(back_window, conv_weight[:, number, :].T, preferred_element_type=jnp.float32)
        conv_term = jnp.stack(conv_terms, axis=1)
        head_term = jnp.dot(active_out.T, head_in, preferred_element_type=jnp.float32)
        normed_flat = normed_in.reshape(cell_count, C)
        inverse_flat = inverse_in.reshape(cell_count, 1)
        input_grad = grad_sum + norm_back(grad_act * silu_slope(normed_flat), normed_flat, inverse_flat)
        input_grad = input_grad.astype(jnp.bfloat16).reshape(FRAMES, H, W, C)
        return ((carry[0] + conv_term, carry[1] + head_term), input_grad)
    initial = (jnp.zeros((C, 27, C), jnp.float32), jnp.zeros((C, 2 * Z), jnp.float32))
    totals, input_grad = lax.scan(one_clip, initial, (block_input, block_output, latent_grad, seeds, lengths))
    return (input_grad, totals[0] * scaling, totals[1] * scaling)
```

```python
import math

import jax
import jax.numpy as jnp
import numpy as np
from jax import lax
from jax.experimental import pallas as pl
from jax.experimental.pallas import tpu as pltpu
from jax.sharding import PartitionSpec as P

MESH = pl.DeviceIdType.MESH
F32 = jnp.float32
BF16 = jnp.bfloat16
EPSILON = 1e-06
ROOT_THREE = math.sqrt(3.0)
SCALING = 1.0 / math.sqrt(131072.0)
C = 384
AXES = ((0, 1, 2), (1, 2, 0), (2, 0, 1))
NT = (((1,), (1,)), ((), ()))
TN = (((0,), (0,)), ((), ()))


def channel_of(x, y, z, core, r):
    return (x // 2) * 192 + y * 48 + z * 12 + core * 6 + (x % 2) * 3 + r


def order_tables():
    tables = np.zeros((3, C, C), np.float32)
    for group, axes in enumerate(AXES):
        for row in range(C):
            place = {axes[0]: row // 96, axes[1]: row // 24 % 4, axes[2]: row // 6 % 4}
            chan = channel_of(place[0], place[1], place[2], row // 3 % 2, row % 3)
            tables[group, row, chan] = 1.0
    return tables


def swap_table():
    table = np.zeros((256, 256), np.float32)
    for tap in range(16):
        for chan in range(16):
            table[tap * 16 + chan, chan * 16 + tap] = 1.0
    return table


def fold_table():
    table = np.zeros((256, 32), np.float32)
    for lane in range(128):
        table[lane, lane % 16] = 1.0
        table[128 + lane, 16 + lane % 16] = 1.0
    return table


def mod(value, base):
    guess = (value.astype(F32) * (1.0 / base)).astype(jnp.int32)
    left = value - guess * base
    left = jnp.where(left < 0, left + base, left)
    return jnp.where(left >= base, left - base, left)


def sigmoid(value):
    return 1.0 / (1.0 + jnp.exp(-value))


def kernel(
    seeds, lengths, bout, lgrad, hw, hwt, binp, wsh, order, swap, fold,
    out_ig, out_cg, out_hg,
    wg, wt, gs, hs, rg, rh, grid, act3, act_t, hpart, hpart_in,
    sb, r1, sum1, r2, p3, r3, fin, fin_in, ybuf,
    ag_s, ag_r, g_s, g_r, gf_s, gf_r, h_s, h_r, hf_s, hf_r, own_sem,
    d2d_s, d2d_r, c1_s, c1_r, c2_s, c2_r, c3_s, c3_r,
):
    dp = lax.axis_index("dp")
    tm = lax.axis_index("tm")
    xl = lax.axis_index("height")
    xh = lax.div(dp, 4)
    y = lax.rem(dp, 4)
    z = lax.div(tm, 2)
    core = lax.rem(tm, 2)
    x = xh * 2 + xl

    def dev(x_, y_, z_, core_):
        return (lax.div(x_, 2) * 4 + y_, z_ * 2 + core_, lax.rem(x_, 2))

    def peer(axis, step):
        place = [x, y, z]
        place[axis] = lax.rem(place[axis] + step, 4)
        return dev(*place, core)

    partner = dev(x, y, z, 1 - core)

    def halo_peer(step):
        return dev(xh * 2 + 1 - xl, y, lax.rem(z + step, 4), core)

    def send(src, dst, s_sem, r_sem, where):
        copy = pltpu.make_async_remote_copy(
            src_ref=src, dst_ref=dst, send_sem=s_sem, recv_sem=r_sem,
            device_id=where, device_id_type=MESH,
        )
        copy.start()
        return copy

    sent = []

    barrier = pltpu.get_barrier_semaphore()
    friends = [peer(axis, step) for axis in range(3) for step in (1, 2, 3)]
    friends.append(partner)
    friends += [halo_peer(step) for step in (1, 2, 3)]
    for friend in friends:
        pl.semaphore_signal(barrier, inc=1, device_id=friend, device_id_type=MESH)
    pl.semaphore_wait(barrier, len(friends))

    ag1 = []
    for half in range(2):
        wg[half, xh, y, z, core, xl] = wsh[half]
        for step in (2, 1, 3):
            n = half * 3 + step - 1
            ag1.append(
                send(wsh.at[half], wg.at[half, xh, y, z, core, xl], ag_s.at[n], ag_r.at[n], peer(2, step))
            )

    gs[16:18] = jnp.zeros((2, 64, C), BF16)
    hs[128:144] = jnp.zeros((16, C), BF16)
    hpart[...] = jnp.zeros((C, 128), F32)
    seed = seeds[0]
    length = lengths[0]

    def head_block(blk, carry):
        rows = pl.multiple_of(blk * 128, 128)
        values = bout[pl.ds(rows, 128), :].astype(F32)
        inverse = lax.rsqrt(jnp.mean(values * values, axis=-1, keepdims=True) + EPSILON)
        normed = values * inverse
        logistic = sigmoid(normed)
        active_out = (normed * logistic).astype(BF16)
        latent = jnp.dot(active_out, hw[...], preferred_element_type=F32)
        lines = pl.multiple_of(blk * 16, 16)
        upstream = lgrad[pl.ds(lines, 16), :]
        line = lax.broadcasted_iota(jnp.int32, (16, 128), 0) + blk * 16
        lane = lax.broadcasted_iota(jnp.int32, (16, 128), 1)
        position = (line + (line >> 3) * 8 + xl * 8) * 1024 + tm * 128 + lane
        primary = mod(seed * 7919 + position, 30269)
        primary = mod(primary * primary + 7, 30269)
        primary = mod(primary * primary + 101, 30269)
        secondary = mod(seed * 7907 + position * 3, 30307)
        secondary = mod(secondary * secondary + 13, 30307)
        secondary = mod(secondary * secondary + 211, 30307)
        combined = mod(primary + secondary, 30269)
        noise = ROOT_THREE * ((combined.astype(F32) + 0.5) * (2.0 / 30269.0) - 1.0)
        pick = lax.broadcasted_iota(jnp.int32, (1, 8, 128), 2) >> 4 == lax.broadcasted_iota(
            jnp.int32, (1, 8, 128), 1
        )

        def spread(part):
            wide = jnp.broadcast_to(part.reshape(16, 1, 128), (16, 8, 128))
            return jnp.where(pick, wide, 0.0).reshape(128, 128)

        both = jnp.concatenate([spread(upstream), spread(0.5 * upstream * noise)], axis=1)
        sides = jnp.dot(both, fold[...], precision=lax.Precision.HIGHEST, preferred_element_type=F32)
        frame = (lax.broadcasted_iota(jnp.int32, (128, 32), 0) >> 6) + blk * 2
        valid = jnp.where(frame < length, 1.0, 0.0)
        is_mean = lax.broadcasted_iota(jnp.int32, (128, 32), 1) < 16
        head_in = valid * jnp.where(
            is_mean, sides + latent, sides * jnp.exp(0.5 * latent) + 0.5 * (jnp.exp(latent) - 1.0)
        )
        head_in = head_in.astype(BF16)
        hpart[:, 0:32] += lax.dot_general(active_out, head_in, TN, preferred_element_type=F32)
        grad = jnp.dot(head_in, hwt[...], preferred_element_type=F32)
        grad = grad * (logistic * (1.0 + normed * (1.0 - logistic)))
        grad = inverse * (grad - normed * jnp.mean(grad * normed, axis=-1, keepdims=True))
        gs[pl.ds(blk * 2, 2)] = grad.astype(BF16).reshape(2, 64, C)
        cells = grad.reshape(2, 8, 8, C)
        border = jnp.where(xl == 0, cells[:, 7], cells[:, 0]).reshape(16, C)
        hs[pl.ds(lines, 16), :] = border.astype(BF16)
        return carry

    lax.fori_loop(0, 8, head_block, 0)

    def frames_of(where):
        return gs.at[pl.ds(where * 4, 6)]

    def border_of(where):
        return hs.at[pl.ds(pl.multiple_of(where * 32, 16), 48), :]

    g_copies = []
    for step in (2, 1, 3):
        g_copies.append(
            send(frames_of(lax.rem(z + step, 4)), rg.at[tm], g_s.at[step], g_r.at[step], peer(2, step))
        )
    g_forward = [send(frames_of(z), rg.at[tm], gf_s.at[0], gf_r.at[0], partner)]
    own = pltpu.make_async_copy(frames_of(z), rg.at[tm], own_sem)
    own.start()
    h_copies = []
    for step in (2, 1, 3, 0):
        h_copies.append(
            send(border_of(lax.rem(z + step, 4)), rh.at[tm], h_s.at[step], h_r.at[step], halo_peer(step))
        )
    hp_copy = send(hpart, hpart_in, d2d_s.at[0], d2d_r.at[0], partner)

    for copy in ag1:
        copy.wait()
    ag2 = []
    for half, axis in ((0, 0), (1, 1)):
        for step in (2, 1, 3):
            n = 6 + half * 3 + step - 1
            held = wg.at[half, xh, y, :, core, xl]
            ag2.append(send(held, held, ag_s.at[n], ag_r.at[n], peer(axis, step)))

    def active_block(blk, carry):
        rows = pl.multiple_of(blk * 64, 64)
        values = binp[pl.ds(rows, 64), :].astype(F32)
        inverse = lax.rsqrt(jnp.mean(values * values, axis=-1, keepdims=True) + EPSILON)
        normed = values * inverse
        active = normed * sigmoid(normed)
        column = lax.broadcasted_iota(jnp.int32, (64, C), 0)
        act3[0, pl.ds(rows, 64), :] = jnp.where(column == 0, 0.0, pltpu.roll(active, 1, 0)).astype(BF16)
        act3[1, pl.ds(rows, 64), :] = active.astype(BF16)
        act3[2, pl.ds(rows, 64), :] = jnp.where(column == 63, 0.0, pltpu.roll(active, 63, 0)).astype(BF16)
        return carry

    lax.fori_loop(0, 16, active_block, 0)
    half_cells = pl.ds(pl.multiple_of(core * 1024, 1024), 1024)
    for group in range(3):
        turned = lax.dot_general(order[group], act3[group], NT, preferred_element_type=F32)
        act_t[group, :, half_cells] = turned.astype(BF16)
    mine = act_t.at[:, :, half_cells]
    act_copy = send(mine, mine, d2d_s.at[1], d2d_r.at[1], partner)

    for copy in ag2:
        copy.wait()
    ag3 = []
    for half, axis in ((0, 1), (1, 0)):
        held = wg.at[0, :, y, :, core, :] if half == 0 else wg.at[1, xh, :, :, core, xl]
        for step in (2, 1, 3):
            n = 12 + half * 3 + step - 1
            ag3.append(send(held, held, ag_s.at[n], ag_r.at[n], peer(axis, step)))

    h_forward = []
    for copy, step in zip(h_copies, (2, 1, 3, 0)):
        copy.wait_recv()
        slot = rh.at[lax.rem(z + 4 - step, 4) * 2 + core]
        h_forward.append(send(slot, slot, hf_s.at[step], hf_r.at[step], partner))
    for copy, step in reversed(list(zip(g_copies, (2, 1, 3)))):
        copy.wait_recv()
        slot = rg.at[lax.rem(z + 4 - step, 4) * 2 + core]
        g_forward.append(send(slot, slot, gf_s.at[step], gf_r.at[step], partner))
    own.wait()
    for copy in g_forward + h_forward:
        copy.wait_recv()

    def place_frame(f, carry):
        for pair in range(4):
            left = rg[2 * pair, f].astype(F32).reshape(8, 8, C)
            right = rg[2 * pair + 1, f].astype(F32).reshape(8, 8, C)
            grid[f, 1:9, pair * 16 : pair * 16 + 16, :] = jnp.concatenate([left, right], axis=1).astype(BF16)
        return carry

    lax.fori_loop(0, 6, place_frame, 0)
    near = 9 - 9 * xl
    for pair in range(4):
        left = rh[2 * pair].astype(F32).reshape(6, 8, C)
        right = rh[2 * pair + 1].astype(F32).reshape(6, 8, C)
        grid[:, near, pair * 16 : pair * 16 + 16, :] = jnp.concatenate([left, right], axis=1).astype(BF16)
    grid[:, 9 - near] = jnp.zeros((6, 64, C), BF16)

    coords = (x, y, z)
    act_copy.wait_recv()

    def window(spot):
        i = lax.div(spot, 3)
        j = lax.rem(spot, 3)
        return grid[pl.ds(2 - i, 4), pl.ds(2 - j, 8)].reshape(2048, C)

    c1 = []

    def scatter(s, group, count):
        axis = AXES[group][0]
        for step in (2, 1, 3):
            target = lax.rem(coords[axis] + step, 4)
            c1.append(
                send(
                    sb.at[s, target, 0:count], r1.at[s, step - 1, 0:count],
                    c1_s.at[s, step - 1], c1_r.at[s, step - 1], peer(axis, step),
                )
            )

    def tap_pairs(u):
        for group in range(3):
            s = 3 * u + group
            first = core * 5 + 2 * u
            both = jnp.concatenate([window(first), window(first + 1)], axis=1)
            res = jnp.dot(act_t[group], both, preferred_element_type=F32).astype(BF16)
            sb[s, :, 0] = res[:, :C].reshape(4, 96, C)
            sb[s, :, 1] = res[:, C:].reshape(4, 96, C)
            scatter(s, group, 2)

    tap_pairs(0)
    for copy in ag3:
        copy.wait()
    held = wg.at[:, :, :, :, core]
    w_copy = send(held, held, d2d_s.at[2], d2d_r.at[2], partner)
    tap_pairs(1)

    def single(group):
        res = jnp.dot(act_t[group], window(4), preferred_element_type=F32)
        sb[6 + group, :, 0] = res.astype(BF16).reshape(4, 96, C)

    hp_copy.wait_recv()

    @pl.when(core == 0)
    def _():
        single(0)
        single(1)
        sb[8, :, 0] = jnp.zeros((4, 96, C), BF16)

    @pl.when(core == 1)
    def _():
        whole = hpart[...] + hpart_in[...]
        ordered = jnp.dot(
            order[0].astype(F32), whole, precision=lax.Precision.HIGHEST, preferred_element_type=F32
        )
        sb[6, :, 0] = jnp.concatenate([ordered, jnp.zeros((C, 256), F32)], axis=1).astype(BF16).reshape(4, 96, C)
        sb[7, :, 0] = jnp.zeros((4, 96, C), BF16)
        single(2)

    for group in range(3):
        scatter(6 + group, group, 1)

    w_copy.wait_recv()

    def turn_weights(blk, carry):
        a = lax.div(blk, 12)
        b = lax.rem(lax.div(blk, 3), 4)
        third = lax.rem(blk, 3)
        rows = pl.multiple_of(blk * 16, 16)
        for half in range(2):
            unit = wt_src(half, a, b, third)
            turned = jnp.dot(swap[...], unit, preferred_element_type=F32).astype(BF16)
            for tap in range(16 if half == 0 else 11):
                k = half * 16 + tap
                spot, group = k // 3, k % 3
                wt[group, pl.ds(rows, 16), spot * C : (spot + 1) * C] = turned[tap * 16 : tap * 16 + 16]
        return carry

    flat = wg.reshape(2, C, 16, C)

    def wt_src(half, a, b, third):
        start = a * 192 + b * 48 + third * 16
        return flat[half, pl.ds(start, 16)].reshape(256, C)

    lax.fori_loop(0, 24, turn_weights, 0)

    weights = wt[...].reshape(3 * C, 9 * C)

    def grad_act(f):
        base = core * 2 + f + 2
        cells = [grid[base - k // 3, 2 - k % 3 : 10 - k % 3].reshape(512, C) for k in range(9)]
        ybuf[f] = lax.dot_general(
            jnp.concatenate(cells, axis=1), weights, NT, preferred_element_type=F32
        )

    grad_act(0)

    for copy in c1:
        copy.wait_recv()
    c2 = []
    for group in range(3):
        lead = coords[AXES[group][0]]
        for u in range(3):
            s = 3 * u + group
            for e in range(2 if u < 2 else 1):
                total = sb[s, lead, e].astype(F32)
                for step in range(3):
                    total = total + r1[s, step, e].astype(F32)
                sum1[group, 2 * u + e] = total
        axis = AXES[group][1]
        for step in (2, 1, 3):
            target = lax.rem(coords[axis] + step, 4)
            c2.append(
                send(
                    sum1.at[group, :, pl.ds(pl.multiple_of(target * 24, 8), 24), :], r2.at[group, step - 1],
                    c2_s.at[group, step - 1], c2_r.at[group, step - 1], peer(axis, step),
                )
            )

    grad_act(1)

    for copy in c2:
        copy.wait_recv()
    c3 = []
    for group in range(3):
        spot = coords[AXES[group][1]]
        for n in range(5):
            total = sum1[group, n, pl.ds(pl.multiple_of(spot * 24, 8), 24), :]
            for step in range(3):
                total = total + r2[group, step, n]
            for a in range(4):
                p3[group, a, n] = jnp.concatenate([total[a * 6 : a * 6 + 6], jnp.zeros((2, C), F32)], axis=0)
        axis = AXES[group][2]
        for step in (2, 1, 3):
            target = lax.rem(coords[axis] + step, 4)
            c3.append(
                send(
                    p3.at[group, target], r3.at[group, step - 1],
                    c3_s.at[group, step - 1], c3_r.at[group, step - 1], peer(axis, step),
                )
            )

    def input_block(blk, carry):
        f = lax.div(blk, 8)
        row = lax.rem(blk, 8)
        rows = pl.multiple_of(blk * 64, 64)
        lines = pl.multiple_of(row * 64, 64)
        values = binp[pl.ds(rows, 64), :].astype(F32)
        inverse = lax.rsqrt(jnp.mean(values * values, axis=-1, keepdims=True) + EPSILON)
        normed = values * inverse
        logistic = sigmoid(normed)
        column = lax.broadcasted_iota(jnp.int32, (64, C), 0)
        after = pltpu.roll(ybuf[f, pl.ds(lines, 64), 0:C], 63, 0)
        before = pltpu.roll(ybuf[f, pl.ds(lines, 64), 2 * C : 3 * C], 1, 0)
        grad = (
            jnp.where(column == 63, 0.0, after)
            + ybuf[f, pl.ds(lines, 64), C : 2 * C]
            + jnp.where(column == 0, 0.0, before)
        )
        grad = grad * (logistic * (1.0 + normed * (1.0 - logistic)))
        grad = inverse * (grad - normed * jnp.mean(grad * normed, axis=-1, keepdims=True))
        direct = grid[core * 2 + f, row + 1].astype(F32)
        out_ig[pl.ds(rows, 64), :] = (direct + grad).astype(BF16)
        return carry

    lax.fori_loop(0, 16, input_block, 0)

    for copy in c3:
        copy.wait_recv()
    for group in range(3):
        spot = coords[AXES[group][2]]
        for n in range(5):
            fin[group, n] = (p3[group, spot, n] + r3[group, 0, n]) + (r3[group, 1, n] + r3[group, 2, n])
    last = send(fin, fin_in, d2d_s.at[3], d2d_r.at[3], partner)
    last.wait_recv()

    def result(holder, group, n):
        value = jnp.where(core == holder, fin[group, n], fin_in[group, n])
        return jnp.where(core == 0, value[0:3], value[3:6]) * SCALING

    for k in range(27):
        if k < 14:
            holder, n = 0, k // 3
        elif k == 14:
            holder, n = 1, 4
        else:
            holder, n = 1, (k - 15) // 3
        out_cg[:, k, :] = result(holder, k % 3, n)
    out_hg[...] = result(1, 0, 4)[:, 0:32]

    for copy in g_copies + g_forward + h_copies + h_forward + c1 + c2 + c3:
        copy.wait_send()
    for copy in (hp_copy, act_copy, w_copy, last):
        copy.wait_send()


def per_device(block_input, block_output, latent_grad, seeds, lengths, conv_weight, head_weight):
    wsh = jnp.pad(conv_weight, ((0, 0), (0, 5), (0, 0))).reshape(3, 2, 16, C).transpose(1, 0, 2, 3)
    order = jnp.asarray(order_tables(), BF16)
    swap = jnp.asarray(swap_table(), BF16)
    fold = jnp.asarray(fold_table(), F32)
    vmem = pl.BlockSpec(memory_space=pltpu.VMEM)
    smem = pl.BlockSpec(memory_space=pltpu.SMEM)
    dma = pltpu.SemaphoreType.DMA
    input_grad, conv_grad, head_grad = pl.pallas_call(
        kernel,
        out_shape=(
            jax.ShapeDtypeStruct((1024, C), BF16),
            jax.ShapeDtypeStruct((3, 27, C), F32),
            jax.ShapeDtypeStruct((3, 32), F32),
        ),
        in_specs=[smem, smem] + [vmem] * 9,
        out_specs=(vmem, vmem, vmem),
        scratch_shapes=[
            pltpu.VMEM((2, 2, 4, 4, 2, 2, 3, 16, C), BF16),
            pltpu.VMEM((3, C, 9 * C), BF16),
            pltpu.VMEM((18, 64, C), BF16),
            pltpu.VMEM((144, C), BF16),
            pltpu.VMEM((8, 6, 64, C), BF16),
            pltpu.VMEM((8, 48, C), BF16),
            pltpu.VMEM((6, 10, 64, C), BF16),
            pltpu.VMEM((3, 1024, C), BF16),
            pltpu.VMEM((3, C, 2048), BF16),
            pltpu.VMEM((C, 128), F32),
            pltpu.VMEM((C, 128), F32),
            pltpu.VMEM((9, 4, 2, 96, C), BF16),
            pltpu.VMEM((9, 3, 2, 96, C), BF16),
            pltpu.VMEM((3, 5, 96, C), F32),
            pltpu.VMEM((3, 3, 5, 24, C), F32),
            pltpu.VMEM((3, 4, 5, 8, C), F32),
            pltpu.VMEM((3, 3, 5, 8, C), F32),
            pltpu.VMEM((3, 5, 8, C), F32),
            pltpu.VMEM((3, 5, 8, C), F32),
            pltpu.VMEM((2, 512, 3 * C), F32),
            dma((18,)), dma((18,)),
            dma((4,)), dma((4,)), dma((4,)), dma((4,)),
            dma((4,)), dma((4,)), dma((4,)), dma((4,)),
            dma,
            dma((4,)), dma((4,)),
            dma((9, 3)), dma((9, 3)),
            dma((3, 3)), dma((3, 3)),
            dma((3, 3)), dma((3, 3)),
        ],
        compiler_params=pltpu.CompilerParams(
            collective_id=0, has_side_effects=True, vmem_limit_bytes=63 * 2**20
        ),
        name="autoencoder_backward",
    )(
        seeds, lengths, block_output.reshape(1024, C), latent_grad.reshape(128, 128),
        head_weight, head_weight.T, block_input.reshape(1024, C), wsh, order, swap, fold,
    )
    return (input_grad.reshape(block_input.shape), conv_grad, head_grad)


def solution(mesh):
    placed = (
        P("dp", "tm", "height", None, None),
        P("dp", None, "height", "tm", None),
        P("dp", None, "height", "tm"),
        P("dp"),
        P("dp"),
        P(("dp", "tm", "height"), None, None),
        P(),
    )
    return jax.shard_map(
        per_device,
        mesh=mesh,
        in_specs=placed,
        out_specs=(
            P("dp", "tm", "height", None, None),
            P(("dp", "tm", "height"), None, None),
            P(("dp", "tm", "height"), None),
        ),
        check_vma=False,
    )
```

```python
import math

import jax
import jax.numpy as jnp
import numpy as np
from jax import lax
from jax.experimental import pallas as pl
from jax.experimental.pallas import tpu as pltpu
from jax.sharding import PartitionSpec as P

MESH = pl.DeviceIdType.MESH
F32 = jnp.float32
BF16 = jnp.bfloat16
EPSILON = 1e-06
ROOT_THREE = math.sqrt(3.0)
SCALING = 1.0 / math.sqrt(131072.0)
C = 384
AXES = ((0, 1, 2), (1, 2, 0), (2, 0, 1))
NT = (((1,), (1,)), ((), ()))
TN = (((0,), (0,)), ((), ()))


def channel_of(x, y, z, core, r):
    return (x // 2) * 192 + y * 48 + z * 12 + core * 6 + (x % 2) * 3 + r


def order_tables():
    tables = np.zeros((3, C, C), np.float32)
    for group, axes in enumerate(AXES):
        for row in range(C):
            place = {axes[0]: row // 96, axes[1]: row // 24 % 4, axes[2]: row // 6 % 4}
            chan = channel_of(place[0], place[1], place[2], row // 3 % 2, row % 3)
            tables[group, row, chan] = 1.0
    return tables


def swap_table():
    table = np.zeros((256, 256), np.float32)
    for tap in range(16):
        for chan in range(16):
            table[tap * 16 + chan, chan * 16 + tap] = 1.0
    return table


def pick_table():
    table = np.zeros((2, 16, 27), np.float32)
    for core in range(2):
        for group in range(3):
            for m in range(5):
                tap = 3 * (4 * core + m) + group
                if (tap >= 14) == (core == 1):
                    table[core, group * 5 + m, tap] = 1.0
    return table


def fold_table():
    table = np.zeros((256, 32), np.float32)
    for lane in range(128):
        table[lane, lane % 16] = 1.0
        table[128 + lane, 16 + lane % 16] = 1.0
    return table


def mod(value, base):
    guess = (value.astype(F32) * (1.0 / base)).astype(jnp.int32)
    left = value - guess * base
    left = jnp.where(left < 0, left + base, left)
    return jnp.where(left >= base, left - base, left)


def sigmoid(value):
    return 1.0 / (1.0 + jnp.exp(-value))


def kernel(
    seeds, lengths, bout, lgrad, hwt, binp, cw, order, swap, fold, pick,
    out_ig, out_cg, out_hg,
    ush, wg, wt, gs, hs, rg, rh, grid, act3, act_t, ao, hin, hpart, hpart_in,
    sb, r1, p2, r2, p3, r3, fin, fin_in, ybuf, part, part_in,
    a1_s, a1_r, a2_s, a2_r, a3_s, a3_r, a4_s, a4_r, g_s, g_r, gf_s, gf_r, h_s, h_r, hf_s, hf_r, own_sem,
    d2d_s, d2d_r, c1_s, c1_r, c2_s, c2_r, c3_s, c3_r,
):
    dp = lax.axis_index("dp")
    tm = lax.axis_index("tm")
    xl = lax.axis_index("height")
    xh = lax.div(dp, 4)
    y = lax.rem(dp, 4)
    z = lax.div(tm, 2)
    core = lax.rem(tm, 2)
    x = xh * 2 + xl

    def dev(x_, y_, z_, core_):
        return (lax.div(x_, 2) * 4 + y_, z_ * 2 + core_, lax.rem(x_, 2))

    def peer(axis, step):
        place = [x, y, z]
        place[axis] = lax.rem(place[axis] + step, 4)
        return dev(*place, core)

    partner = dev(x, y, z, 1 - core)

    def halo_peer(step):
        return dev(xh * 2 + 1 - xl, y, lax.rem(z + step, 4), core)

    def across(step):
        return dev(x, y, lax.rem(z + step, 4), 1 - core)

    def send(src, dst, s_sem, r_sem, where):
        copy = pltpu.make_async_remote_copy(
            src_ref=src, dst_ref=dst, send_sem=s_sem, recv_sem=r_sem,
            device_id=where, device_id_type=MESH,
        )
        copy.start()
        return copy

    barrier = pltpu.get_barrier_semaphore()
    friends = [peer(axis, step) for axis in range(3) for step in (1, 2, 3)]
    friends += [across(step) for step in range(4)]
    friends += [halo_peer(step) for step in (1, 2, 3)]
    for friend in friends:
        pl.semaphore_signal(barrier, inc=1, device_id=friend, device_id_type=MESH)

    for taps in range(2):
        for r in range(3):
            ush[taps, r] = jnp.dot(pick[taps], cw[r], preferred_element_type=F32).astype(BF16)

    gs[16:18] = jnp.zeros((2, 64, C), BF16)
    hs[128:144] = jnp.zeros((16, C), BF16)
    seed = seeds[0]
    length = lengths[0]

    def head_block(turn, carry):
        blk = lax.rem(turn + 2 * z + 2, 8)
        rows = pl.multiple_of(blk * 128, 128)
        values = bout[pl.ds(rows, 128), :].astype(F32)
        inverse = lax.rsqrt(jnp.mean(values * values, axis=-1, keepdims=True) + EPSILON)
        normed = values * inverse
        logistic = sigmoid(normed)
        active_out = (normed * logistic).astype(BF16)
        latent = lax.dot_general(active_out, hwt[...], NT, preferred_element_type=F32)
        lines = pl.multiple_of(blk * 16, 16)
        upstream = lgrad[pl.ds(lines, 16), :]
        line = lax.broadcasted_iota(jnp.int32, (16, 128), 0) + blk * 16
        lane = lax.broadcasted_iota(jnp.int32, (16, 128), 1)
        position = (line + (line >> 3) * 8 + xl * 8) * 1024 + tm * 128 + lane
        primary = mod(seed * 7919 + position, 30269)
        primary = mod(primary * primary + 7, 30269)
        primary = mod(primary * primary + 101, 30269)
        secondary = mod(seed * 7907 + position * 3, 30307)
        secondary = mod(secondary * secondary + 13, 30307)
        secondary = mod(secondary * secondary + 211, 30307)
        combined = mod(primary + secondary, 30269)
        noise = ROOT_THREE * ((combined.astype(F32) + 0.5) * (2.0 / 30269.0) - 1.0)
        pick = lax.broadcasted_iota(jnp.int32, (1, 8, 128), 2) >> 4 == lax.broadcasted_iota(
            jnp.int32, (1, 8, 128), 1
        )

        def spread(part):
            wide = jnp.broadcast_to(part.reshape(16, 1, 128), (16, 8, 128))
            return jnp.where(pick, wide, 0.0).reshape(128, 128)

        both = jnp.concatenate([spread(upstream), spread(0.5 * upstream * noise)], axis=1)
        sides = jnp.dot(both, fold[...], precision=lax.Precision.HIGHEST, preferred_element_type=F32)
        frame = (lax.broadcasted_iota(jnp.int32, (128, 32), 0) >> 6) + blk * 2
        valid = jnp.where(frame < length, 1.0, 0.0)
        is_mean = lax.broadcasted_iota(jnp.int32, (128, 32), 1) < 16
        head_in = valid * jnp.where(
            is_mean, sides + latent, sides * jnp.exp(0.5 * latent) + 0.5 * (jnp.exp(latent) - 1.0)
        )
        head_in = head_in.astype(BF16)
        ao[pl.ds(rows, 128), :] = active_out
        hin[pl.ds(rows, 128), :] = head_in
        grad = jnp.dot(head_in, hwt[...], preferred_element_type=F32)
        grad = grad * (logistic * (1.0 + normed * (1.0 - logistic)))
        grad = inverse * (grad - normed * jnp.mean(grad * normed, axis=-1, keepdims=True))
        gs[pl.ds(blk * 2, 2)] = grad.astype(BF16).reshape(2, 64, C)
        cells = grad.reshape(2, 8, 8, C)
        border = jnp.where(xl == 0, cells[:, 7], cells[:, 0]).reshape(16, C)
        hs[pl.ds(lines, 16), :] = border.astype(BF16)
        return carry

    def frames_of(where):
        return gs.at[pl.ds(where * 4, 6)]

    def border_of(where):
        return hs.at[pl.ds(pl.multiple_of(where * 32, 16), 48), :]

    g_copies = []
    h_copies = []

    def send_frames(step):
        target = lax.rem(z + step, 4)
        g_copies.append(send(frames_of(target), rg.at[tm], g_s.at[step], g_r.at[step], peer(2, step)))
        h_copies.append(send(border_of(target), rh.at[tm], h_s.at[step], h_r.at[step], halo_peer(step)))

    lax.fori_loop(0, 1, head_block, 0)
    pl.semaphore_wait(barrier, len(friends))

    ag1 = []
    here = wg.at[xh, y, z, core, xl]
    wg[xh, y, z, core, xl] = ush[core]
    for step in (2, 1, 3):
        ag1.append(send(ush.at[core], here, a1_s.at[step], a1_r.at[step], peer(2, step)))
    for step in (0, 2, 1, 3):
        ag1.append(send(ush.at[1 - core], here, a1_s.at[4 + step], a1_r.at[4 + step], across(step)))

    lax.fori_loop(1, 3, head_block, 0)
    send_frames(1)
    lax.fori_loop(3, 5, head_block, 0)
    send_frames(2)
    lax.fori_loop(5, 7, head_block, 0)
    send_frames(3)
    lax.fori_loop(7, 8, head_block, 0)
    g_forward = [send(frames_of(z), rg.at[tm], gf_s.at[0], gf_r.at[0], partner)]
    own = pltpu.make_async_copy(frames_of(z), rg.at[tm], own_sem)
    own.start()
    h_copies.append(send(border_of(z), rh.at[tm], h_s.at[0], h_r.at[0], halo_peer(0)))

    routes = ((0, 1), (1, 0))

    def chunk(half, near, far):
        place = [x, y]
        place[routes[half][0]] = lax.rem(place[routes[half][0]] + 4 - near, 4)
        place[routes[half][1]] = lax.rem(place[routes[half][1]] + 4 - far, 4)
        return wg.at[lax.div(place[0], 2), place[1], :, half, lax.rem(place[0], 2)]

    ag2 = {}
    ag3 = {}
    ag4 = {}

    def pass_on(half, j):
        block = chunk(half, j, 0)
        for way, step in ((0, 1), (1, 3)):
            ag3[half, j, way] = send(
                block, block, a3_s.at[half, j, way], a3_r.at[half, j, way], peer(routes[half][1], step)
            )

    def relay(j):
        way, step = (0, 1) if j % 2 == 0 else (1, 3)
        for half in range(2):
            ag3[half, j, way].wait_recv()
            block = chunk(half, j, step)
            ag4[half, j] = send(
                block, block, a4_s.at[half, j], a4_r.at[half, j], peer(routes[half][1], step)
            )

    for copy in ag1:
        copy.wait()
    for half in range(2):
        block = chunk(half, 0, 0)
        for step in (2, 1, 3):
            n = step - 1
            ag2[half, step] = send(
                block, block, a2_s.at[half, n], a2_r.at[half, n], peer(routes[half][0], step)
            )
        pass_on(half, 0)

    hpart[...] = jnp.zeros((C, 128), F32)
    hpart[:, 0:32] = lax.dot_general(ao[...], hin[...], TN, preferred_element_type=F32)
    hp_copy = send(hpart, hpart_in, d2d_s.at[0], d2d_r.at[0], partner)

    def active_block(blk, carry):
        rows = pl.multiple_of(blk * 64, 64)
        values = binp[pl.ds(rows, 64), :].astype(F32)
        inverse = lax.rsqrt(jnp.mean(values * values, axis=-1, keepdims=True) + EPSILON)
        normed = values * inverse
        active = normed * sigmoid(normed)
        column = lax.broadcasted_iota(jnp.int32, (64, C), 0)
        act3[0, pl.ds(rows, 64), :] = jnp.where(column == 0, 0.0, pltpu.roll(active, 1, 0)).astype(BF16)
        act3[1, pl.ds(rows, 64), :] = active.astype(BF16)
        act3[2, pl.ds(rows, 64), :] = jnp.where(column == 63, 0.0, pltpu.roll(active, 63, 0)).astype(BF16)
        return carry

    lax.fori_loop(0, 16, active_block, 0)
    half_cells = pl.ds(pl.multiple_of(core * 1024, 1024), 1024)
    for group in range(3):
        turned = lax.dot_general(order[group], act3[group], NT, preferred_element_type=F32)
        act_t[group, :, half_cells] = turned.astype(BF16)
    mine = act_t.at[:, :, half_cells]
    act_copy = send(mine, mine, d2d_s.at[1], d2d_r.at[1], partner)

    for step in (1, 3, 2):
        for half in range(2):
            ag2[half, step].wait_recv()
            pass_on(half, step)

    hp_copy.wait_recv()

    @pl.when(core == 1)
    def _():
        whole = hpart[...] + hpart_in[...]
        ordered = jnp.zeros((C, 128), F32)
        for _ in range(3):
            piece = whole.astype(BF16)
            ordered += jnp.dot(order[0], piece, preferred_element_type=F32)
            whole = whole - piece.astype(F32)
        sb[6, :, 0] = jnp.concatenate([ordered, jnp.zeros((C, 256), F32)], axis=1).astype(BF16).reshape(4, 96, C)

    relay(0)
    h_forward = []
    for g_copy, h_copy, step in zip(g_copies + [None], h_copies, (1, 2, 3, 0)):
        slot = lax.rem(z + 4 - step, 4) * 2 + core
        if g_copy is not None:
            g_copy.wait_recv()
            g_forward.append(send(rg.at[slot], rg.at[slot], gf_s.at[step], gf_r.at[step], partner))
        h_copy.wait_recv()
        h_forward.append(send(rh.at[slot], rh.at[slot], hf_s.at[step], hf_r.at[step], partner))
    relay(1)
    relay(3)
    own.wait()
    for copy in g_forward + h_forward:
        copy.wait_recv()

    def place_frame(f, carry):
        for pair in range(4):
            left = rg[2 * pair, f].astype(F32).reshape(8, 8, C)
            right = rg[2 * pair + 1, f].astype(F32).reshape(8, 8, C)
            grid[f, 1:9, pair * 16 : pair * 16 + 16, :] = jnp.concatenate([left, right], axis=1).astype(BF16)
        return carry

    lax.fori_loop(0, 6, place_frame, 0)
    near = 9 - 9 * xl
    for pair in range(4):
        left = rh[2 * pair].astype(F32).reshape(6, 8, C)
        right = rh[2 * pair + 1].astype(F32).reshape(6, 8, C)
        grid[:, near, pair * 16 : pair * 16 + 16, :] = jnp.concatenate([left, right], axis=1).astype(BF16)
    grid[:, 9 - near] = jnp.zeros((6, 64, C), BF16)

    coords = (x, y, z)
    act_copy.wait_recv()

    def window(spot):
        i = lax.div(spot, 3)
        j = lax.rem(spot, 3)
        return grid[pl.ds(2 - i, 4), pl.ds(2 - j, 8)].reshape(2048, C)

    def scatter(s, group, count):
        axis = AXES[group][0]
        copies = []
        for step in (2, 1, 3):
            target = lax.rem(coords[axis] + step, 4)
            copies.append(
                pltpu.make_async_remote_copy(
                    src_ref=sb.at[s, target, 0:count], dst_ref=r1.at[s, step - 1, 0:count],
                    send_sem=c1_s.at[s, step - 1], recv_sem=c1_r.at[s, step - 1],
                    device_id=peer(axis, step), device_id_type=MESH,
                )
            )
        return copies

    def tap_pairs(u):
        for group in range(3):
            s = 3 * u + group
            first = core * 5 + 2 * u
            both = jnp.concatenate([window(first), window(first + 1)], axis=1)
            res = jnp.dot(act_t[group], both, preferred_element_type=F32).astype(BF16)
            sb[s, :, 0] = res[:, :C].reshape(4, 96, C)
            sb[s, :, 1] = res[:, C:].reshape(4, 96, C)
            for copy in scatter(s, group, 2):
                copy.start()

    users = (None, 0, 1)

    def for_user(group, act):
        if users[group] is None:
            act()
        else:
            pl.when(core == users[group])(act)

    def single(group):
        res = jnp.dot(act_t[group], window(4), preferred_element_type=F32)
        sb[6 + group, :, 0] = res.astype(BF16).reshape(4, 96, C)

    def start_single(group):
        for copy in scatter(6 + group, group, 1):
            copy.start()

    tap_pairs(0)
    relay(2)
    tap_pairs(1)
    pl.when(core == 0)(lambda: single(0))
    start_single(0)
    for group in (1, 2):

        def last_taps(group=group):
            single(group)
            start_single(group)

        for_user(group, last_taps)

    for half in range(2):
        for j in range(4):
            ag3[half, j, 0].wait_recv() if j % 2 else None
            ag3[half, j, 1].wait_recv() if j % 2 == 0 else None
            ag4[half, j].wait_recv()
    flat = wg.reshape(C, 16, C)

    def turn_weights(blk, carry):
        rows = pl.multiple_of(blk * 16, 16)
        unit = flat[pl.ds(rows, 16)].reshape(256, C)
        turned = jnp.dot(swap[...], unit, preferred_element_type=F32).astype(BF16)
        for group in range(3):
            for m in range(5):
                row = (group * 5 + m) * 16
                wt[group, pl.ds(rows, 16), m * C : (m + 1) * C] = turned[row : row + 16]
        return carry

    lax.fori_loop(0, 24, turn_weights, 0, unroll=4)

    weights = wt[...].reshape(3 * C, 5 * C)

    def grad_act(owner):
        cells = []
        for m in range(5):
            spot = 4 * core + m
            i = lax.div(spot, 3)
            j = lax.rem(spot, 3)
            cells.append(grid[pl.ds(owner * 2 + 2 - i, 2), pl.ds(2 - j, 8)].reshape(1024, C))
        ybuf[...] = lax.dot_general(
            jnp.concatenate(cells, axis=1), weights, NT, preferred_element_type=F32
        )

    def shifted(rows):
        column = lax.broadcasted_iota(jnp.int32, (64, C), 0)
        after = pltpu.roll(ybuf[pl.ds(rows, 64), 0:C], 63, 0)
        before = pltpu.roll(ybuf[pl.ds(rows, 64), 2 * C : 3 * C], 1, 0)
        return (
            jnp.where(column == 63, 0.0, after)
            + ybuf[pl.ds(rows, 64), C : 2 * C]
            + jnp.where(column == 0, 0.0, before)
        )

    grad_act(1 - core)

    def part_block(row, carry):
        rows = pl.multiple_of(row * 64, 64)
        part[pl.ds(rows, 64), :] = shifted(rows)
        return carry

    lax.fori_loop(0, 16, part_block, 0)
    part_copy = send(part, part_in, d2d_s.at[2], d2d_r.at[2], partner)

    for s in range(6):
        for copy in scatter(s, s % 3, 2):
            copy.wait_recv()
    for group in range(3):

        def arrived(group=group):
            for copy in scatter(6 + group, group, 1):
                copy.wait_recv()

        for_user(group, arrived)

    c2 = []
    for group in range(3):
        lead = coords[AXES[group][0]]
        if users[group] is not None:

            def blank(group=group):
                sb[6 + group, lead, 0] = jnp.zeros((96, C), BF16)
                for step in range(3):
                    r1[6 + group, step, 0] = jnp.zeros((96, C), BF16)

            pl.when(core != users[group])(blank)
        for a in range(4):
            lines = slice(a * 24, a * 24 + 24)
            totals = []
            for n in range(5):
                s = 3 * (n // 2) + group
                total = sb[s, lead, n % 2, lines].astype(F32)
                for step in range(3):
                    total = total + r1[s, step, n % 2, lines].astype(F32)
                totals.append(total)
            totals.append(jnp.zeros((8, C), F32))
            p2[group, a] = jnp.concatenate(totals, axis=0).astype(BF16)
        axis = AXES[group][1]
        for step in (2, 1, 3):
            target = lax.rem(coords[axis] + step, 4)
            c2.append(
                send(
                    p2.at[group, target], r2.at[group, step - 1],
                    c2_s.at[group, step - 1], c2_r.at[group, step - 1], peer(axis, step),
                )
            )

    grad_act(core)

    for copy in c2:
        copy.wait_recv()
    c3 = []
    for group in range(3):
        spot = coords[AXES[group][1]]
        total = p2[group, spot].astype(F32)
        for step in range(3):
            total = total + r2[group, step].astype(F32)
        for a in range(4):
            rows = [total[n * 24 + a * 6 : n * 24 + a * 6 + 6] for n in range(5)]
            p3[group, a] = jnp.concatenate(rows + [jnp.zeros((2, C), F32)], axis=0).astype(BF16)
        axis = AXES[group][2]
        for step in (2, 1, 3):
            target = lax.rem(coords[axis] + step, 4)
            c3.append(
                send(
                    p3.at[group, target], r3.at[group, step - 1],
                    c3_s.at[group, step - 1], c3_r.at[group, step - 1], peer(axis, step),
                )
            )

    def input_block(blk, carry):
        f = lax.div(blk, 8)
        row = lax.rem(blk, 8)
        rows = pl.multiple_of(blk * 64, 64)
        values = binp[pl.ds(rows, 64), :].astype(F32)
        inverse = lax.rsqrt(jnp.mean(values * values, axis=-1, keepdims=True) + EPSILON)
        normed = values * inverse
        logistic = sigmoid(normed)
        grad = shifted(rows) + part_in[pl.ds(rows, 64), :]
        grad = grad * (logistic * (1.0 + normed * (1.0 - logistic)))
        grad = inverse * (grad - normed * jnp.mean(grad * normed, axis=-1, keepdims=True))
        direct = grid[core * 2 + f, row + 1].astype(F32)
        out_ig[pl.ds(rows, 64), :] = (direct + grad).astype(BF16)
        return carry

    part_copy.wait_recv()
    lax.fori_loop(0, 16, input_block, 0)

    for copy in c3:
        copy.wait_recv()
    for group in range(3):
        spot = coords[AXES[group][2]]
        total = p3[group, spot].astype(F32)
        for step in range(3):
            total = total + r3[group, step].astype(F32)
        fin[group] = total
    last = send(fin, fin_in, d2d_s.at[3], d2d_r.at[3], partner)
    last.wait_recv()

    def result(holder, group, n):
        value = jnp.where(core == holder, fin[group, n * 6 : n * 6 + 6], fin_in[group, n * 6 : n * 6 + 6])
        return jnp.where(core == 0, value[0:3], value[3:6]) * SCALING

    for k in range(27):
        if k < 14:
            holder, n = 0, k // 3
        elif k == 14:
            holder, n = 1, 4
        else:
            holder, n = 1, (k - 15) // 3
        out_cg[:, k, :] = result(holder, k % 3, n)
    out_hg[...] = result(1, 0, 4)[:, 0:32]

    for copy in g_copies + g_forward + h_copies + h_forward + c2 + c3:
        copy.wait_send()
    for s in range(6):
        for copy in scatter(s, s % 3, 2):
            copy.wait_send()
    for group in range(3):

        def left(group=group):
            for copy in scatter(6 + group, group, 1):
                copy.wait_send()

        for_user(group, left)
    for copy in (*ag2.values(), *ag3.values(), *ag4.values(), hp_copy, act_copy, part_copy, last):
        copy.wait_send()


def per_device(block_input, block_output, latent_grad, seeds, lengths, conv_weight, head_weight):
    order = jnp.asarray(order_tables(), BF16)
    swap = jnp.asarray(swap_table(), BF16)
    fold = jnp.asarray(fold_table(), F32)
    pick = jnp.asarray(pick_table(), BF16)
    vmem = pl.BlockSpec(memory_space=pltpu.VMEM)
    smem = pl.BlockSpec(memory_space=pltpu.SMEM)
    dma = pltpu.SemaphoreType.DMA
    input_grad, conv_grad, head_grad = pl.pallas_call(
        kernel,
        out_shape=(
            jax.ShapeDtypeStruct((1024, C), BF16),
            jax.ShapeDtypeStruct((3, 27, C), F32),
            jax.ShapeDtypeStruct((3, 32), F32),
        ),
        in_specs=[smem, smem] + [vmem] * 9,
        out_specs=(vmem, vmem, vmem),
        scratch_shapes=[
            pltpu.VMEM((2, 3, 16, C), BF16),
            pltpu.VMEM((2, 4, 4, 2, 2, 3, 16, C), BF16),
            pltpu.VMEM((3, C, 5 * C), BF16),
            pltpu.VMEM((18, 64, C), BF16),
            pltpu.VMEM((144, C), BF16),
            pltpu.VMEM((8, 6, 64, C), BF16),
            pltpu.VMEM((8, 48, C), BF16),
            pltpu.VMEM((6, 10, 64, C), BF16),
            pltpu.VMEM((3, 1024, C), BF16),
            pltpu.VMEM((3, C, 2048), BF16),
            pltpu.VMEM((1024, C), BF16),
            pltpu.VMEM((1024, 32), BF16),
            pltpu.VMEM((C, 128), F32),
            pltpu.VMEM((C, 128), F32),
            pltpu.VMEM((9, 4, 2, 96, C), BF16),
            pltpu.VMEM((9, 3, 2, 96, C), BF16),
            pltpu.VMEM((3, 4, 128, C), BF16),
            pltpu.VMEM((3, 3, 128, C), BF16),
            pltpu.VMEM((3, 4, 32, C), BF16),
            pltpu.VMEM((3, 3, 32, C), BF16),
            pltpu.VMEM((3, 32, C), F32),
            pltpu.VMEM((3, 32, C), F32),
            pltpu.VMEM((1024, 3 * C), F32),
            pltpu.VMEM((1024, C), F32),
            pltpu.VMEM((1024, C), F32),
            dma((8,)), dma((8,)), dma((2, 3)), dma((2, 3)),
            dma((2, 4, 2)), dma((2, 4, 2)), dma((2, 4)), dma((2, 4)),
            dma((4,)), dma((4,)), dma((4,)), dma((4,)),
            dma((4,)), dma((4,)), dma((4,)), dma((4,)),
            dma,
            dma((4,)), dma((4,)),
            dma((9, 3)), dma((9, 3)),
            dma((3, 3)), dma((3, 3)),
            dma((3, 3)), dma((3, 3)),
        ],
        compiler_params=pltpu.CompilerParams(
            collective_id=0, has_side_effects=True, vmem_limit_bytes=63 * 2**20
        ),
        name="autoencoder_backward",
    )(
        seeds, lengths, block_output.reshape(1024, C), latent_grad.reshape(128, 128),
        head_weight.T, block_input.reshape(1024, C), conv_weight, order, swap, fold, pick,
    )
    return (input_grad.reshape(block_input.shape), conv_grad, head_grad)


def solution(mesh):
    placed = (
        P("dp", "tm", "height", None, None),
        P("dp", None, "height", "tm", None),
        P("dp", None, "height", "tm"),
        P("dp"),
        P("dp"),
        P(("dp", "tm", "height"), None, None),
        P(),
    )
    return jax.shard_map(
        per_device,
        mesh=mesh,
        in_specs=placed,
        out_specs=(
            P("dp", "tm", "height", None, None),
            P(("dp", "tm", "height"), None, None),
            P(("dp", "tm", "height"), None),
        ),
        check_vma=False,
    )
```

```python
import math

import jax
import jax.numpy as jnp
import numpy as np
from jax import lax
from jax.experimental import pallas as pl
from jax.experimental.pallas import tpu as pltpu
from jax.sharding import PartitionSpec as P

MESH = pl.DeviceIdType.MESH
F32 = jnp.float32
BF16 = jnp.bfloat16
EPSILON = 1e-06
ROOT_THREE = math.sqrt(3.0)
SCALING = 1.0 / math.sqrt(131072.0)
C = 384
AXES = ((0, 1, 2), (1, 2, 0), (2, 0, 1))
NT = (((1,), (1,)), ((), ()))
TN = (((0,), (0,)), ((), ()))


def channel_of(x, y, z, core, r):
    return (x // 2) * 192 + y * 48 + z * 12 + core * 6 + (x % 2) * 3 + r


def order_tables():
    tables = np.zeros((3, C, C), np.float32)
    for group, axes in enumerate(AXES):
        for row in range(C):
            place = {axes[0]: row // 96, axes[1]: row // 24 % 4, axes[2]: row // 6 % 4}
            chan = channel_of(place[0], place[1], place[2], row // 3 % 2, row % 3)
            tables[group, row, chan] = 1.0
    return tables


def swap_table():
    table = np.zeros((256, 256), np.float32)
    for tap in range(16):
        for chan in range(16):
            table[tap * 16 + chan, chan * 16 + tap] = 1.0
    return table


def pick_table():
    table = np.zeros((2, 16, 27), np.float32)
    for core in range(2):
        for group in range(3):
            for m in range(5):
                tap = 3 * (4 * core + m) + group
                if (tap >= 14) == (core == 1):
                    table[core, group * 5 + m, tap] = 1.0
    return table


def fold_table():
    table = np.zeros((256, 32), np.float32)
    for lane in range(128):
        table[lane, lane % 16] = 1.0
        table[128 + lane, 16 + lane % 16] = 1.0
    return table


def mod(value, base):
    guess = (value.astype(F32) * (1.0 / base)).astype(jnp.int32)
    left = value - guess * base
    left = jnp.where(left < 0, left + base, left)
    return jnp.where(left >= base, left - base, left)


def sigmoid(value):
    return 1.0 / (1.0 + jnp.exp(-value))


def kernel(
    seeds, lengths, bout, lgrad, hwt, binp, cw, order, swap, fold, pick,
    out_ig, out_cg, out_hg,
    ush, wg, wt, gs, hs, rg, rh, grid, act3, act_t, ao, hin, hpart, hpart_in,
    sb, r1, p2, r2, p3, r3, r4, fin, fin_in, ybuf, part, part_in,
    a1_s, a1_r, a2_s, a2_r, a3_s, a3_r, a4_s, a4_r, g_s, g_r, gf_s, gf_r, h_s, h_r, hf_s, hf_r, own_sem,
    d2d_s, d2d_r, c1_s, c1_r, c2_s, c2_r, c3_s, c3_r, c4_s, c4_r,
):
    dp = lax.axis_index("dp")
    tm = lax.axis_index("tm")
    xl = lax.axis_index("height")
    xh = lax.div(dp, 4)
    y = lax.rem(dp, 4)
    z = lax.div(tm, 2)
    core = lax.rem(tm, 2)
    x = xh * 2 + xl

    def dev(x_, y_, z_, core_):
        return (lax.div(x_, 2) * 4 + y_, z_ * 2 + core_, lax.rem(x_, 2))

    def peer(axis, step):
        place = [x, y, z]
        place[axis] = lax.rem(place[axis] + step, 4)
        return dev(*place, core)

    partner = dev(x, y, z, 1 - core)

    def halo_peer(step):
        return dev(xh * 2 + 1 - xl, y, lax.rem(z + step, 4), core)

    def across(axis, step):
        place = [x, y, z]
        place[axis] = lax.rem(place[axis] + step, 4)
        return dev(*place, 1 - core)

    def send(src, dst, s_sem, r_sem, where):
        copy = pltpu.make_async_remote_copy(
            src_ref=src, dst_ref=dst, send_sem=s_sem, recv_sem=r_sem,
            device_id=where, device_id_type=MESH,
        )
        copy.start()
        return copy

    barrier = pltpu.get_barrier_semaphore()
    friends = [peer(axis, step) for axis in range(3) for step in (1, 2, 3)]
    friends += [partner] + [across(axis, step) for axis in range(3) for step in (1, 2, 3)]
    friends += [halo_peer(step) for step in (1, 2, 3)]
    for friend in friends:
        pl.semaphore_signal(barrier, inc=1, device_id=friend, device_id_type=MESH)

    for taps in range(2):
        for r in range(3):
            ush[taps, r] = jnp.dot(pick[taps], cw[r], preferred_element_type=F32).astype(BF16)

    gs[16:18] = jnp.zeros((2, 64, C), BF16)
    hs[128:144] = jnp.zeros((16, C), BF16)
    seed = seeds[0]
    length = lengths[0]

    def head_block(turn, carry):
        blk = lax.rem(turn + 2 * z + 2, 8)
        rows = pl.multiple_of(blk * 128, 128)
        values = bout[pl.ds(rows, 128), :].astype(F32)
        inverse = lax.rsqrt(jnp.mean(values * values, axis=-1, keepdims=True) + EPSILON)
        normed = values * inverse
        logistic = sigmoid(normed)
        active_out = (normed * logistic).astype(BF16)
        latent = lax.dot_general(active_out, hwt[...], NT, preferred_element_type=F32)
        lines = pl.multiple_of(blk * 16, 16)
        upstream = lgrad[pl.ds(lines, 16), :]
        line = lax.broadcasted_iota(jnp.int32, (16, 128), 0) + blk * 16
        lane = lax.broadcasted_iota(jnp.int32, (16, 128), 1)
        position = (line + (line >> 3) * 8 + xl * 8) * 1024 + tm * 128 + lane
        primary = mod(seed * 7919 + position, 30269)
        primary = mod(primary * primary + 7, 30269)
        primary = mod(primary * primary + 101, 30269)
        secondary = mod(seed * 7907 + position * 3, 30307)
        secondary = mod(secondary * secondary + 13, 30307)
        secondary = mod(secondary * secondary + 211, 30307)
        combined = mod(primary + secondary, 30269)
        noise = ROOT_THREE * ((combined.astype(F32) + 0.5) * (2.0 / 30269.0) - 1.0)
        pick = lax.broadcasted_iota(jnp.int32, (1, 8, 128), 2) >> 4 == lax.broadcasted_iota(
            jnp.int32, (1, 8, 128), 1
        )

        def spread(part):
            wide = jnp.broadcast_to(part.reshape(16, 1, 128), (16, 8, 128))
            return jnp.where(pick, wide, 0.0).reshape(128, 128)

        both = jnp.concatenate([spread(upstream), spread(0.5 * upstream * noise)], axis=1)
        sides = jnp.dot(both, fold[...], precision=lax.Precision.HIGHEST, preferred_element_type=F32)
        frame = (lax.broadcasted_iota(jnp.int32, (128, 32), 0) >> 6) + blk * 2
        valid = jnp.where(frame < length, 1.0, 0.0)
        is_mean = lax.broadcasted_iota(jnp.int32, (128, 32), 1) < 16
        head_in = valid * jnp.where(
            is_mean, sides + latent, sides * jnp.exp(0.5 * latent) + 0.5 * (jnp.exp(latent) - 1.0)
        )
        head_in = head_in.astype(BF16)
        ao[pl.ds(rows, 128), :] = active_out
        hin[pl.ds(rows, 128), :] = head_in
        grad = jnp.dot(head_in, hwt[...], preferred_element_type=F32)
        grad = grad * (logistic * (1.0 + normed * (1.0 - logistic)))
        grad = inverse * (grad - normed * jnp.mean(grad * normed, axis=-1, keepdims=True))
        gs[pl.ds(blk * 2, 2)] = grad.astype(BF16).reshape(2, 64, C)
        cells = grad.reshape(2, 8, 8, C)
        border = jnp.where(xl == 0, cells[:, 7], cells[:, 0]).reshape(16, C)
        hs[pl.ds(lines, 16), :] = border.astype(BF16)
        return carry

    def frames_of(where):
        return gs.at[pl.ds(where * 4, 6)]

    def border_of(where):
        return hs.at[pl.ds(pl.multiple_of(where * 32, 16), 48), :]

    g_copies = []
    h_copies = []

    def send_frames(step):
        target = lax.rem(z + step, 4)
        g_copies.append(send(frames_of(target), rg.at[tm], g_s.at[step], g_r.at[step], peer(2, step)))
        h_copies.append(send(border_of(target), rh.at[tm], h_s.at[step], h_r.at[step], halo_peer(step)))

    lax.fori_loop(0, 1, head_block, 0)
    pl.semaphore_wait(barrier, len(friends))

    ag1 = []
    here = wg.at[xh, y, z, core, xl]
    wg[xh, y, z, core, xl] = ush[core]
    for step in (2, 1, 3):
        ag1.append(send(ush.at[core], here, a1_s.at[step], a1_r.at[step], peer(2, step)))
    for step in (0, 2, 1, 3):
        ag1.append(send(ush.at[1 - core], here, a1_s.at[4 + step], a1_r.at[4 + step], across(2, step)))

    lax.fori_loop(1, 3, head_block, 0)
    send_frames(1)
    lax.fori_loop(3, 5, head_block, 0)
    send_frames(2)
    lax.fori_loop(5, 7, head_block, 0)
    send_frames(3)
    lax.fori_loop(7, 8, head_block, 0)
    g_forward = [send(frames_of(z), rg.at[tm], gf_s.at[0], gf_r.at[0], partner)]
    own = pltpu.make_async_copy(frames_of(z), rg.at[tm], own_sem)
    own.start()
    h_copies.append(send(border_of(z), rh.at[tm], h_s.at[0], h_r.at[0], halo_peer(0)))

    routes = ((0, 1), (1, 0))

    def chunk(half, near, far):
        place = [x, y]
        place[routes[half][0]] = lax.rem(place[routes[half][0]] + 4 - near, 4)
        place[routes[half][1]] = lax.rem(place[routes[half][1]] + 4 - far, 4)
        return wg.at[lax.div(place[0], 2), place[1], :, half, lax.rem(place[0], 2)]

    ag2 = {}
    ag3 = {}
    ag4 = {}

    def pass_on(half, j):
        block = chunk(half, j, 0)
        for way, step in ((0, 1), (1, 3)):
            ag3[half, j, way] = send(
                block, block, a3_s.at[half, j, way], a3_r.at[half, j, way], peer(routes[half][1], step)
            )

    def relay(j):
        way, step = (0, 1) if j % 2 == 0 else (1, 3)
        for half in range(2):
            ag3[half, j, way].wait_recv()
            block = chunk(half, j, step)
            ag4[half, j] = send(
                block, block, a4_s.at[half, j], a4_r.at[half, j], peer(routes[half][1], step)
            )

    for copy in ag1:
        copy.wait()
    for half in range(2):
        block = chunk(half, 0, 0)
        for step in (2, 1, 3):
            n = step - 1
            ag2[half, step] = send(
                block, block, a2_s.at[half, n], a2_r.at[half, n], peer(routes[half][0], step)
            )
        pass_on(half, 0)

    hpart[...] = jnp.zeros((C, 128), F32)
    hpart[:, 0:32] = lax.dot_general(ao[...], hin[...], TN, preferred_element_type=F32)
    hp_copy = send(hpart, hpart_in, d2d_s.at[0], d2d_r.at[0], partner)

    def active_block(blk, carry):
        rows = pl.multiple_of(blk * 64, 64)
        values = binp[pl.ds(rows, 64), :].astype(F32)
        inverse = lax.rsqrt(jnp.mean(values * values, axis=-1, keepdims=True) + EPSILON)
        normed = values * inverse
        active = normed * sigmoid(normed)
        column = lax.broadcasted_iota(jnp.int32, (64, C), 0)
        act3[0, pl.ds(rows, 64), :] = jnp.where(column == 0, 0.0, pltpu.roll(active, 1, 0)).astype(BF16)
        act3[1, pl.ds(rows, 64), :] = active.astype(BF16)
        act3[2, pl.ds(rows, 64), :] = jnp.where(column == 63, 0.0, pltpu.roll(active, 63, 0)).astype(BF16)
        return carry

    lax.fori_loop(0, 16, active_block, 0)
    half_cells = pl.ds(pl.multiple_of(core * 1024, 1024), 1024)
    for group in range(3):
        turned = lax.dot_general(order[group], act3[group], NT, preferred_element_type=F32)
        act_t[group, :, half_cells] = turned.astype(BF16)
    mine = act_t.at[:, :, half_cells]
    act_copy = send(mine, mine, d2d_s.at[1], d2d_r.at[1], partner)

    for step in (1, 3, 2):
        for half in range(2):
            ag2[half, step].wait_recv()
            pass_on(half, step)

    hp_copy.wait_recv()

    @pl.when(core == 1)
    def _():
        whole = hpart[...] + hpart_in[...]
        ordered = jnp.zeros((C, 128), F32)
        for _ in range(3):
            piece = whole.astype(BF16)
            ordered += jnp.dot(order[0], piece, preferred_element_type=F32)
            whole = whole - piece.astype(F32)
        sb[6, :, 0] = jnp.concatenate([ordered, jnp.zeros((C, 256), F32)], axis=1).astype(BF16).reshape(4, 96, C)

    relay(0)
    h_forward = []
    for g_copy, h_copy, step in zip(g_copies + [None], h_copies, (1, 2, 3, 0)):
        slot = lax.rem(z + 4 - step, 4) * 2 + core
        if g_copy is not None:
            g_copy.wait_recv()
            g_forward.append(send(rg.at[slot], rg.at[slot], gf_s.at[step], gf_r.at[step], partner))
            if step == 1:
                relay(1)
            if step == 2:
                relay(3)
        h_copy.wait_recv()
        h_forward.append(send(rh.at[slot], rh.at[slot], hf_s.at[step], hf_r.at[step], partner))
    relay(2)
    own.wait()
    for copy in g_forward + h_forward:
        copy.wait_recv()

    def place_frame(f, carry):
        for pair in range(4):
            left = rg[2 * pair, f].astype(F32).reshape(8, 8, C)
            right = rg[2 * pair + 1, f].astype(F32).reshape(8, 8, C)
            grid[f, 1:9, pair * 16 : pair * 16 + 16, :] = jnp.concatenate([left, right], axis=1).astype(BF16)
        return carry

    lax.fori_loop(0, 6, place_frame, 0)
    near = 9 - 9 * xl
    for pair in range(4):
        left = rh[2 * pair].astype(F32).reshape(6, 8, C)
        right = rh[2 * pair + 1].astype(F32).reshape(6, 8, C)
        grid[:, near, pair * 16 : pair * 16 + 16, :] = jnp.concatenate([left, right], axis=1).astype(BF16)
    grid[:, 9 - near] = jnp.zeros((6, 64, C), BF16)

    coords = (x, y, z)
    act_copy.wait_recv()

    def window(spot):
        i = lax.div(spot, 3)
        j = lax.rem(spot, 3)
        return grid[pl.ds(2 - i, 4), pl.ds(2 - j, 8)].reshape(2048, C)

    def scatter(s, group, count):
        axis = AXES[group][0]
        copies = []
        for step in (2, 1, 3):
            target = lax.rem(coords[axis] + step, 4)
            copies.append(
                pltpu.make_async_remote_copy(
                    src_ref=sb.at[s, target, 0:count], dst_ref=r1.at[s, step - 1, 0:count],
                    send_sem=c1_s.at[s, step - 1], recv_sem=c1_r.at[s, step - 1],
                    device_id=peer(axis, step), device_id_type=MESH,
                )
            )
        return copies

    def tap_pairs(u):
        for group in range(3):
            s = 3 * u + group
            first = core * 5 + 2 * u
            both = jnp.concatenate([window(first), window(first + 1)], axis=1)
            res = jnp.dot(act_t[group], both, preferred_element_type=F32).astype(BF16)
            sb[s, :, 0] = res[:, :C].reshape(4, 96, C)
            sb[s, :, 1] = res[:, C:].reshape(4, 96, C)
            for copy in scatter(s, group, 2):
                copy.start()

    users = (None, 0, 1)

    def for_user(group, act):
        if users[group] is None:
            act()
        else:
            pl.when(core == users[group])(act)

    def single(group):
        res = jnp.dot(act_t[group], window(4), preferred_element_type=F32)
        sb[6 + group, :, 0] = res.astype(BF16).reshape(4, 96, C)

    def start_single(group):
        for copy in scatter(6 + group, group, 1):
            copy.start()

    tap_pairs(0)
    tap_pairs(1)
    pl.when(core == 0)(lambda: single(0))
    start_single(0)
    for group in (1, 2):

        def last_taps(group=group):
            single(group)
            start_single(group)

        for_user(group, last_taps)

    for half in range(2):
        for j in range(4):
            ag3[half, j, 0].wait_recv() if j % 2 else None
            ag3[half, j, 1].wait_recv() if j % 2 == 0 else None
            ag4[half, j].wait_recv()
    flat = wg.reshape(C, 16, C)

    def turn_weights(blk, carry):
        rows = pl.multiple_of(blk * 16, 16)
        unit = flat[pl.ds(rows, 16)].reshape(256, C)
        turned = jnp.dot(swap[...], unit, preferred_element_type=F32).astype(BF16)
        for group in range(3):
            for m in range(5):
                row = (group * 5 + m) * 16
                wt[group, pl.ds(rows, 16), m * C : (m + 1) * C] = turned[row : row + 16]
        return carry

    lax.fori_loop(0, 24, turn_weights, 0, unroll=4)

    weights = wt.reshape(3 * C, 5 * C)

    def grad_act(owner):
        def of_core(number):
            cells = []
            for m in range(5):
                i, j = divmod(4 * number + m, 3)
                cells.append(grid[pl.ds(owner * 2 + 2 - i, 2), 2 - j : 10 - j].reshape(1024, C))
            cells = jnp.concatenate(cells, axis=1)
            first = slice(0, 5 * C) if number == 0 else slice(C, 5 * C)
            last = slice(0, 4 * C) if number == 0 else slice(0, 5 * C)
            ybuf[:, : 2 * C] = lax.dot_general(
                cells[:, first], weights[: 2 * C, first], NT, preferred_element_type=F32
            )
            ybuf[:, 2 * C :] = lax.dot_general(
                cells[:, last], weights[2 * C :, last], NT, preferred_element_type=F32
            )

        pl.when(core == 0)(lambda: of_core(0))
        pl.when(core == 1)(lambda: of_core(1))

    def shifted(rows):
        column = lax.broadcasted_iota(jnp.int32, (64, C), 0)
        after = pltpu.roll(ybuf[pl.ds(rows, 64), 0:C], 63, 0)
        before = pltpu.roll(ybuf[pl.ds(rows, 64), 2 * C : 3 * C], 1, 0)
        return (
            jnp.where(column == 63, 0.0, after)
            + ybuf[pl.ds(rows, 64), C : 2 * C]
            + jnp.where(column == 0, 0.0, before)
        )

    grad_act(1 - core)

    def part_block(row, carry):
        rows = pl.multiple_of(row * 64, 64)
        part[pl.ds(rows, 64), :] = shifted(rows)
        return carry

    lax.fori_loop(0, 16, part_block, 0)
    part_copy = send(part, part_in, d2d_s.at[2], d2d_r.at[2], partner)

    for s in range(6):
        for copy in scatter(s, s % 3, 2):
            copy.wait_recv()
    for group in range(3):

        def arrived(group=group):
            for copy in scatter(6 + group, group, 1):
                copy.wait_recv()

        for_user(group, arrived)

    c2 = []
    for group in range(3):
        lead = coords[AXES[group][0]]
        if users[group] is not None:

            def blank(group=group):
                sb[6 + group, lead, 0] = jnp.zeros((96, C), BF16)
                for step in range(3):
                    r1[6 + group, step, 0] = jnp.zeros((96, C), BF16)

            pl.when(core != users[group])(blank)
        for a in range(4):
            lines = slice(a * 24, a * 24 + 24)
            totals = []
            for n in range(5):
                s = 3 * (n // 2) + group
                total = sb[s, lead, n % 2, lines].astype(F32)
                for step in range(3):
                    total = total + r1[s, step, n % 2, lines].astype(F32)
                totals.append(total)
            totals.append(jnp.zeros((8, C), F32))
            p2[group, a] = jnp.concatenate(totals, axis=0).astype(BF16)
        axis = AXES[group][1]
        for step in (2, 1, 3):
            target = lax.rem(coords[axis] + step, 4)
            c2.append(
                send(
                    p2.at[group, target], r2.at[group, step - 1],
                    c2_s.at[group, step - 1], c2_r.at[group, step - 1], peer(axis, step),
                )
            )

    grad_act(core)

    for copy in c2:
        copy.wait_recv()
    c3 = []
    for group in range(3):
        spot = coords[AXES[group][1]]
        total = p2[group, spot].astype(F32)
        for step in range(3):
            total = total + r2[group, step].astype(F32)
        for a in range(4):
            rows = [total[n * 24 + a * 6 : n * 24 + a * 6 + 6] for n in range(5)]
            p3[group, a] = jnp.concatenate(rows + [jnp.zeros((2, C), F32)], axis=0).astype(BF16)
        axis = AXES[group][2]
        for step in (2, 1, 3, 0):
            target = lax.rem(coords[axis] + step, 4)
            c3.append(
                send(
                    p3.at[group, target], r4.at[group, step],
                    c4_s.at[group, step], c4_r.at[group, step], across(axis, step),
                )
            )
            if step == 0:
                continue
            c3.append(
                send(
                    p3.at[group, target], r3.at[group, step - 1],
                    c3_s.at[group, step - 1], c3_r.at[group, step - 1], peer(axis, step),
                )
            )

    def input_block(blk, carry):
        f = lax.div(blk, 8)
        row = lax.rem(blk, 8)
        rows = pl.multiple_of(blk * 64, 64)
        values = binp[pl.ds(rows, 64), :].astype(F32)
        inverse = lax.rsqrt(jnp.mean(values * values, axis=-1, keepdims=True) + EPSILON)
        normed = values * inverse
        logistic = sigmoid(normed)
        grad = shifted(rows) + part_in[pl.ds(rows, 64), :]
        grad = grad * (logistic * (1.0 + normed * (1.0 - logistic)))
        grad = inverse * (grad - normed * jnp.mean(grad * normed, axis=-1, keepdims=True))
        direct = grid[core * 2 + f, row + 1].astype(F32)
        out_ig[pl.ds(rows, 64), :] = (direct + grad).astype(BF16)
        return carry

    part_copy.wait_recv()
    lax.fori_loop(0, 16, input_block, 0)

    for copy in c3:
        copy.wait_recv()
    for group in range(3):
        spot = coords[AXES[group][2]]
        total = p3[group, spot].astype(F32)
        for step in range(3):
            total = total + r3[group, step].astype(F32)
        fin[group] = total
        total = r4[group, 0].astype(F32)
        for step in (1, 2, 3):
            total = total + r4[group, step].astype(F32)
        fin_in[group] = total

    def result(holder, group, n):
        value = jnp.where(core == holder, fin[group, n * 6 : n * 6 + 6], fin_in[group, n * 6 : n * 6 + 6])
        return jnp.where(core == 0, value[0:3], value[3:6]) * SCALING

    for k in range(27):
        if k < 14:
            holder, n = 0, k // 3
        elif k == 14:
            holder, n = 1, 4
        else:
            holder, n = 1, (k - 15) // 3
        out_cg[:, k, :] = result(holder, k % 3, n)
    out_hg[...] = result(1, 0, 4)[:, 0:32]

    for copy in g_copies + g_forward + h_copies + h_forward + c2 + c3:
        copy.wait_send()
    for s in range(6):
        for copy in scatter(s, s % 3, 2):
            copy.wait_send()
    for group in range(3):

        def left(group=group):
            for copy in scatter(6 + group, group, 1):
                copy.wait_send()

        for_user(group, left)
    for copy in (*ag2.values(), *ag3.values(), *ag4.values(), hp_copy, act_copy, part_copy):
        copy.wait_send()


def per_device(block_input, block_output, latent_grad, seeds, lengths, conv_weight, head_weight):
    order = jnp.asarray(order_tables(), BF16)
    swap = jnp.asarray(swap_table(), BF16)
    fold = jnp.asarray(fold_table(), F32)
    pick = jnp.asarray(pick_table(), BF16)
    vmem = pl.BlockSpec(memory_space=pltpu.VMEM)
    smem = pl.BlockSpec(memory_space=pltpu.SMEM)
    dma = pltpu.SemaphoreType.DMA
    input_grad, conv_grad, head_grad = pl.pallas_call(
        kernel,
        out_shape=(
            jax.ShapeDtypeStruct((1024, C), BF16),
            jax.ShapeDtypeStruct((3, 27, C), F32),
            jax.ShapeDtypeStruct((3, 32), F32),
        ),
        in_specs=[smem, smem] + [vmem] * 9,
        out_specs=(vmem, vmem, vmem),
        scratch_shapes=[
            pltpu.VMEM((2, 3, 16, C), BF16),
            pltpu.VMEM((2, 4, 4, 2, 2, 3, 16, C), BF16),
            pltpu.VMEM((3, C, 5 * C), BF16),
            pltpu.VMEM((18, 64, C), BF16),
            pltpu.VMEM((144, C), BF16),
            pltpu.VMEM((8, 6, 64, C), BF16),
            pltpu.VMEM((8, 48, C), BF16),
            pltpu.VMEM((6, 10, 64, C), BF16),
            pltpu.VMEM((3, 1024, C), BF16),
            pltpu.VMEM((3, C, 2048), BF16),
            pltpu.VMEM((1024, C), BF16),
            pltpu.VMEM((1024, 32), BF16),
            pltpu.VMEM((C, 128), F32),
            pltpu.VMEM((C, 128), F32),
            pltpu.VMEM((9, 4, 2, 96, C), BF16),
            pltpu.VMEM((9, 3, 2, 96, C), BF16),
            pltpu.VMEM((3, 4, 128, C), BF16),
            pltpu.VMEM((3, 3, 128, C), BF16),
            pltpu.VMEM((3, 4, 32, C), BF16),
            pltpu.VMEM((3, 3, 32, C), BF16),
            pltpu.VMEM((3, 4, 32, C), BF16),
            pltpu.VMEM((3, 32, C), F32),
            pltpu.VMEM((3, 32, C), F32),
            pltpu.VMEM((1024, 3 * C), F32),
            pltpu.VMEM((1024, C), F32),
            pltpu.VMEM((1024, C), F32),
            dma((8,)), dma((8,)), dma((2, 3)), dma((2, 3)),
            dma((2, 4, 2)), dma((2, 4, 2)), dma((2, 4)), dma((2, 4)),
            dma((4,)), dma((4,)), dma((4,)), dma((4,)),
            dma((4,)), dma((4,)), dma((4,)), dma((4,)),
            dma,
            dma((4,)), dma((4,)),
            dma((9, 3)), dma((9, 3)),
            dma((3, 3)), dma((3, 3)),
            dma((3, 3)), dma((3, 3)),
            dma((3, 4)), dma((3, 4)),
        ],
        compiler_params=pltpu.CompilerParams(
            collective_id=0, has_side_effects=True, vmem_limit_bytes=63 * 2**20
        ),
        name="autoencoder_backward",
    )(
        seeds, lengths, block_output.reshape(1024, C), latent_grad.reshape(128, 128),
        head_weight.T, block_input.reshape(1024, C), conv_weight, order, swap, fold, pick,
    )
    return (input_grad.reshape(block_input.shape), conv_grad, head_grad)


def solution(mesh):
    placed = (
        P("dp", "tm", "height", None, None),
        P("dp", None, "height", "tm", None),
        P("dp", None, "height", "tm"),
        P("dp"),
        P("dp"),
        P(("dp", "tm", "height"), None, None),
        P(),
    )
    return jax.shard_map(
        per_device,
        mesh=mesh,
        in_specs=placed,
        out_specs=(
            P("dp", "tm", "height", None, None),
            P(("dp", "tm", "height"), None, None),
            P(("dp", "tm", "height"), None),
        ),
        check_vma=False,
    )
```
